32 devices in a mesh: grp: 2 (over x), seq: 8 (over z, y), head: 2 (over core).
Axes of the slice: x: 2, y: 2, z: 4, core: 2. Of those that a mesh axis runs over, the one named last changes fastest.
Arguments:
- queries: bfloat16 [16384, 2048], P(('grp', 'seq'), 'head'), parts along dimension 0, may hold values from -6 to 6
- key_states: bfloat16 [16384, 1024], P(('grp', 'seq'), 'head'), parts along dimension 0, may hold values from -6 to 6
- value_states: bfloat16 [16384, 1024], P(('grp', 'seq'), 'head'), parts along dimension 0, may hold values from -6 to 6
- segment_ids: int32 [16384], P(('grp', 'seq')), parts along dimension 0, may hold values from 0 to 15, as said below
Outputs:
- attended: bfloat16 [16384, 2048], P(('grp', 'seq'), 'head'), parts along dimension 0
The draws below stay inside these ranges and needn't reach their ends.
There are 2 independent parts, one for each index of `grp`. The reference program is written for one: setup_inputs(seed, part) draws one part's arguments, and reference() takes and returns one part's arrays. A program takes and returns all parts, laid end to end along the dimension named above; each array names one. Nothing has to cross between parts.
Inputs may be any that keep to these rules, and one draw needn't show every extreme that they name: `segment_ids`: read in logical order, the ids never fall, start at 0 and name all 16 candidates, each one token or more; the first 1536 and the last 1536 logical tokens each lie within one candidate.
All inputs are finite; a program needn't handle non-finite values.
Results may differ from the reference program's by a relative error of at most 0.008.
Values may be sent and summed in bfloat16 or wider, within the bound.
A program may use at most 64 MiB of HBM per device.

```python
import jax
import jax.numpy as jnp
from jax import lax

HEAD_DIM = 128
QHEADS = 16
KVHEADS = 8
WINDOW = 1024
TOK_DEV = 1024
TOKENS = 8192
CANDS = 16
N_SEQ = 8


def draw_queries(key, part):
    shape_all = (TOKENS, QHEADS * HEAD_DIM)
    return jax.random.truncated_normal(jax.random.fold_in(key, 1), -6.0, 6.0, shape_all, jnp.float32).astype(jnp.bfloat16)


def draw_key_states(key, part):
    shape_all = (TOKENS, KVHEADS * HEAD_DIM)
    return jax.random.truncated_normal(jax.random.fold_in(key, 2), -6.0, 6.0, shape_all, jnp.float32).astype(jnp.bfloat16)


def draw_segment_ids(key, part):
    span_rows = TOK_DEV // 2
    seq_count = TOKENS // TOK_DEV
    room = TOKENS - 6 * span_rows + 1
    starts = jax.random.permutation(jax.random.fold_in(key, 3), room)[:CANDS - 1] + 3 * span_rows
    flags = jnp.zeros((TOKENS,), jnp.int32).at[starts].set(1)
    logical = jnp.cumsum(flags).astype(jnp.int32)
    blocks = logical.reshape(2 * seq_count, span_rows)
    return jnp.stack([blocks[:seq_count], blocks[seq_count:][::-1]], axis=1).reshape(TOKENS)


def level_of(rng, shape, pieces, least, largest):
    factor_of, own = 1.0, jax.random.fold_in(rng, 6)
    for dim, parts in pieces:
        draws = jnp.exp(jax.random.uniform(jax.random.fold_in(own, dim), (parts,), jnp.float32, least / len(pieces), largest / len(pieces)))
        factor_of = factor_of * jnp.repeat(draws, shape[dim] // parts).reshape([-1 if axis == dim else 1 for axis in range(len(shape))])
    return factor_of


def centred(rng, dims, scale, bound, split=(), kind=jnp.bfloat16):
    gain = level_of(rng, dims, split, -0.22, 0.18) if split else 1.0
    values = jax.random.normal(rng, dims, jnp.float32) * scale * gain
    return jnp.minimum(jnp.maximum(values, -bound), bound).astype(kind)


def setup_inputs(seed: int = 0, part: int = 0) -> dict:
    arg_keys = jax.random.split(jax.random.key(seed), 5)
    own_keys = jax.random.split(jax.random.fold_in(arg_keys[4], part), 5)
    return {
        "queries": draw_queries(jax.random.fold_in(jax.random.fold_in(arg_keys[4], part), 71), part),
        "key_states": draw_key_states(jax.random.fold_in(jax.random.fold_in(arg_keys[4], part), 71), part),
        "value_states": centred(own_keys[2], (TOKENS, KVHEADS * HEAD_DIM), 1.0, 6.0, ((0, 8), (1, 2))),
        "segment_ids": draw_segment_ids(jax.random.fold_in(jax.random.fold_in(arg_keys[4], part), 71), part),
    }


attn_scale = 168.0 ** -0.5


def reference(queries, key_states, value_states, segment_ids):
    span_rows = TOK_DEV // 2
    seq_count = N_SEQ
    groups = QHEADS // KVHEADS

    def unfold(stored):
        blocks = stored.reshape((seq_count, 2, span_rows) + stored.shape[1:])
        return jnp.concatenate([blocks[:, 0], blocks[::-1, 1]], axis=0).reshape(stored.shape)

    def refold(logical):
        blocks = logical.reshape((2 * seq_count, span_rows) + logical.shape[1:])
        return jnp.stack([blocks[:seq_count], blocks[seq_count:][::-1]], axis=1).reshape(logical.shape)

    query_log = unfold(queries)
    key_log = jnp.concatenate([jnp.zeros((2 * span_rows, key_states.shape[1]), key_states.dtype), unfold(key_states)], axis=0)
    value_log = jnp.concatenate([jnp.zeros((2 * span_rows, value_states.shape[1]), value_states.dtype), unfold(value_states)], axis=0)
    seg_log = unfold(segment_ids)
    seg_pad = jnp.concatenate([jnp.full((2 * span_rows,), -1, jnp.int32), seg_log.astype(jnp.int32)], axis=0)

    def one_span(block):
        start = (block * span_rows).astype(jnp.int32)
        query_blk = lax.dynamic_slice_in_dim(query_log, start, span_rows, 0)
        key_blk = lax.dynamic_slice_in_dim(key_log, start, 3 * span_rows, 0)
        value_blk = lax.dynamic_slice_in_dim(value_log, start, 3 * span_rows, 0)
        query_seg = lax.dynamic_slice_in_dim(seg_log, start, span_rows, 0)
        key_seg = lax.dynamic_slice_in_dim(seg_pad, start, 3 * span_rows, 0)
        query_pos = start + jnp.arange(span_rows, dtype=jnp.int32)
        key_pos = start - 2 * span_rows + jnp.arange(3 * span_rows, dtype=jnp.int32)
        visible = (key_pos[None, :] <= query_pos[:, None]) & (key_pos[None, :] > query_pos[:, None] - WINDOW)
        visible = visible & (key_pos[None, :] >= 0) & (key_seg[None, :] == query_seg[:, None])
        query_four = query_blk.astype(jnp.float32).reshape(span_rows, KVHEADS, groups, HEAD_DIM)
        key_three = key_blk.astype(jnp.float32).reshape(3 * span_rows, KVHEADS, HEAD_DIM)
        value_three = value_blk.astype(jnp.float32).reshape(3 * span_rows, KVHEADS, HEAD_DIM)
        scores = jnp.einsum("qhgd,khd->hgqk", query_four, key_three) * attn_scale
        scores = jnp.where(visible[None, None], scores, jnp.float32(-1e30))
        row_max = jnp.max(scores, axis=-1, keepdims=True)
        exp_terms = jnp.exp(scores - row_max)
        weights = (exp_terms / jnp.sum(exp_terms, axis=-1, keepdims=True)).astype(jnp.bfloat16)
        mixed_out = jnp.einsum("hgqk,khd->qhgd", weights.astype(jnp.float32), value_three)
        return mixed_out.astype(jnp.bfloat16).reshape(span_rows, QHEADS * HEAD_DIM)

    outputs = lax.map(one_span, jnp.arange(2 * seq_count, dtype=jnp.int32))
    return refold(outputs.reshape(2 * seq_count * span_rows, QHEADS * HEAD_DIM))
```

```python
import functools

import jax
import jax.numpy as jnp
from jax import lax
from jax.experimental import pallas as pl
from jax.experimental.pallas import tpu as pltpu
from jax.sharding import PartitionSpec as P

HEAD_DIM = 128
WINDOW = 1024
LANES = 128
TILE = 256
MESH = pl.DeviceIdType.MESH

SCALE2 = (168.0 ** (-0.5)) * 1.4426950408889634
NEG = -1e30

OWN_F, OWN_B, FP1, FP2, BN1, BN2 = range(6)


def kernel(n, kv_heads, groups, q_hbm, k_hbm, v_hbm, seg_ref, o_hbm,
           kv, q_vm, o_vm, segs, lo,
           send_sem, recv_sem, seg_send, seg_recv, own_sem, q_sem, o_sem):
    me = lax.axis_index("seq")
    half = q_vm.shape[0] // 2
    rows_seg = half // LANES

    offsets = (1, 2, -1, -2)
    slots = (FP1, FP2, BN1, BN2)

    def exists(off):
        return (me + off >= 0) & (me + off < n)

    barrier = pltpu.get_barrier_semaphore()
    for off in offsets:
        @pl.when(exists(off))
        def _():
            pl.semaphore_signal(barrier, inc=1, device_id={"seq": me + off}, device_id_type=MESH)
    peers = sum(exists(off).astype(jnp.int32) for off in offsets)
    pl.semaphore_wait(barrier, peers)

    def seg_copy(j):
        return pltpu.make_async_remote_copy(
            src_ref=seg_ref, dst_ref=segs.at[j], send_sem=seg_send.at[j], recv_sem=seg_recv.at[j],
            device_id={"seq": me + offsets[j]}, device_id_type=MESH)

    def part(ref, row, h):
        return ref.at[pl.ds(row, half), pl.ds(pl.multiple_of(h * HEAD_DIM, HEAD_DIM), HEAD_DIM)]

    def kv_copy(j, which, h, off=None, row=None):
        off = offsets[j] if off is None else off
        row = (0 if j < 2 else half) if row is None else row
        return pltpu.make_async_remote_copy(
            src_ref=part((k_hbm, v_hbm)[which], row, h), dst_ref=kv.at[slots[j], which, h],
            send_sem=send_sem.at[j, which, h], recv_sem=recv_sem.at[j, which, h],
            device_id={"seq": me + off}, device_id_type=MESH)

    def edge_copy(which, h):
        return pltpu.make_async_remote_copy(
            src_ref=part((k_hbm, v_hbm)[which], 0, h), dst_ref=kv.at[BN2, which, h],
            send_sem=send_sem.at[4, which, h], recv_sem=recv_sem.at[3, which, h],
            device_id={"seq": me - 1}, device_id_type=MESH)

    def start_sends(h):
        for j in range(4):
            @pl.when(exists(offsets[j]))
            def _():
                for which in range(2):
                    kv_copy(j, which, h).start()

        @pl.when(me == n - 1)
        def _():
            for which in range(2):
                edge_copy(which, h).start()

    def wait_sends(h):
        for j in range(4):
            @pl.when(exists(offsets[j]))
            def _():
                for which in range(2):
                    kv_copy(j, which, h).wait_send()

        @pl.when(me == n - 1)
        def _():
            for which in range(2):
                edge_copy(which, h).wait_send()

    def wait_recvs(h):
        for j, there in enumerate((me >= 1, me >= 2, me <= n - 2, me <= n - 2)):
            @pl.when(there)
            def _():
                for which in range(2):
                    kv_copy(j, which, h).wait_recv()

    def own_copy(b, which, h):
        return pltpu.make_async_copy(
            part((k_hbm, v_hbm)[which], b * half, h), kv.at[b, which, h], own_sem.at[b, which, h])

    for j in range(4):
        @pl.when(exists(offsets[j]))
        def _():
            seg_copy(j).start()
    start_sends(0)
    start_sends(1)
    q_copy = pltpu.make_async_copy(q_hbm, q_vm, q_sem)
    q_copy.start()
    for h in range(kv_heads):
        for b in range(2):
            for which in range(2):
                own_copy(b, which, h).start()

    for slot, missing in ((FP1, me < 1), (FP2, me < 2)):
        @pl.when(missing)
        def _():
            kv[slot] = jnp.zeros(kv.shape[1:], kv.dtype)
            segs[slot - FP1] = jnp.full(segs.shape[1:], -1, segs.dtype)

    segs[4] = seg_ref[...]
    for j in range(4):
        there = exists(-offsets[j])

        @pl.when(there)
        def _():
            seg_copy(j).wait_recv()

    last = me == n - 1
    second = me == n - 2
    seg_places = (
        ((1, 0), (0, 0), (4, 0)),
        (
            (jnp.where(last, 0, jnp.where(second, 2, 3)), jnp.where(last | second, 0, rows_seg)),
            (jnp.where(last, 4, 2), jnp.where(last, 0, rows_seg)),
            (4, rows_seg),
        ),
    )
    for b in range(2):
        band = []
        for slot, row in seg_places[b]:
            for c in range(rows_seg):
                band.append(segs[slot, pl.ds(row + c, 1), :])
        for c in range(rows_seg):
            own = band[2 * rows_seg + c]
            own_col = jnp.transpose(jnp.broadcast_to(own, (LANES, LANES)))
            count = jnp.zeros((LANES, LANES), jnp.float32)
            for keys in band:
                count = count + jnp.where(keys < own_col, 1.0, 0.0)
            first = jnp.sum(count, axis=1, keepdims=True).astype(jnp.int32)
            row_of = lax.broadcasted_iota(jnp.int32, (LANES, LANES), 0) + (c * LANES + 1)
            lo[b, pl.ds(c * LANES, LANES), :] = jnp.maximum(jnp.broadcast_to(first, (LANES, LANES)), row_of)

    q_copy.wait()

    def out_copy(h):
        cols = pl.ds(pl.multiple_of(h * groups * HEAD_DIM, HEAD_DIM), groups * HEAD_DIM)
        return pltpu.make_async_copy(o_vm.at[:, cols], o_hbm.at[:, cols], o_sem.at[h])

    def attend(h, b, g):
        older1 = jnp.where(b == 0, FP1, jnp.where(last, OWN_F, BN1))
        older2 = jnp.where(b == 0, FP2, jnp.where(last, FP1, BN2))
        col = pl.multiple_of((h * groups + g) * HEAD_DIM, HEAD_DIM)
        for t in range(half // TILE):
            row = pl.multiple_of(b * half + t * TILE, TILE)
            q = q_vm[pl.ds(row, TILE), pl.ds(col, HEAD_DIM)]
            low = lo[b, pl.ds(t * TILE, TILE), 0:1]
            pieces = (
                (older2, t * TILE, half - t * TILE, t * TILE),
                (older1, 0, half, half),
                (b, 0, (t + 1) * TILE, 2 * half),
            )
            scores = []
            for p, (slot, k0, kn, base) in enumerate(pieces):
                k = kv[slot, 0, h, pl.ds(k0, kn), :]
                s = lax.dot_general(q, k, (((1,), (1,)), ((), ())), preferred_element_type=jnp.float32)
                key_at = lax.broadcasted_iota(jnp.int32, (TILE, kn), 1) + base
                seen = key_at >= low
                if p == 2:
                    row_at = lax.broadcasted_iota(jnp.int32, (TILE, kn), 0) + (2 * half + t * TILE)
                    seen = seen & (key_at <= row_at)
                scores.append(jnp.where(seen, s * SCALE2, NEG))
            top = functools.reduce(jnp.maximum, [jnp.max(s, axis=1, keepdims=True) for s in scores])
            acc = None
            for s, (slot, k0, kn, base) in zip(scores, pieces):
                w = jnp.exp2(s - top).astype(jnp.bfloat16)
                v = kv[slot, 1, h, pl.ds(k0, kn), :]
                v = jnp.concatenate([v, jnp.ones((kn, LANES), jnp.bfloat16)], axis=1)
                d = lax.dot_general(w, v, (((1,), (0,)), ((), ())), preferred_element_type=jnp.float32)
                acc = d if acc is None else acc + d
            o_vm[pl.ds(row, TILE), pl.ds(col, HEAD_DIM)] = (
                acc[:, :HEAD_DIM] / acc[:, HEAD_DIM:]).astype(o_vm.dtype)

    def head_step(h, carry):
        for b in range(2):
            for which in range(2):
                own_copy(b, which, h).wait()
        wait_recvs(h)

        @pl.when(h + 2 < kv_heads)
        def _():
            start_sends(h + 2)

        def one(i, c):
            attend(h, i // groups, i % groups)
            return c

        lax.fori_loop(0, 2 * groups, one, 0)
        out_copy(h).start()
        return carry

    lax.fori_loop(0, kv_heads, head_step, 0)

    for j in range(4):
        @pl.when(exists(offsets[j]))
        def _():
            seg_copy(j).wait_send()

    def finish(h, carry):
        wait_sends(h)
        out_copy(h).wait()
        return carry

    lax.fori_loop(0, kv_heads, finish, 0)


def body(queries, key_states, value_states, segment_ids):
    rows, q_cols = queries.shape
    half = rows // 2
    kv_heads = key_states.shape[1] // HEAD_DIM
    groups = q_cols // key_states.shape[1]
    n = lax.axis_size("seq")
    seg_tile = segment_ids.reshape(rows // LANES, LANES)
    anywhere = pl.BlockSpec(memory_space=pl.ANY)
    flops = 4 * rows * q_cols * 5 * TILE
    return pl.pallas_call(
        functools.partial(kernel, n, kv_heads, groups),
        out_shape=jax.ShapeDtypeStruct((rows, q_cols), jnp.bfloat16),
        in_specs=[anywhere, anywhere, anywhere, pl.BlockSpec(memory_space=pltpu.VMEM)],
        out_specs=anywhere,
        scratch_shapes=[
            pltpu.VMEM((6, 2, kv_heads, half, HEAD_DIM), jnp.bfloat16),
            pltpu.VMEM((rows, q_cols), jnp.bfloat16),
            pltpu.VMEM((rows, q_cols), jnp.bfloat16),
            pltpu.VMEM((5, rows // LANES, LANES), jnp.int32),
            pltpu.VMEM((2, half, LANES), jnp.int32),
            pltpu.SemaphoreType.DMA((5, 2, kv_heads)),
            pltpu.SemaphoreType.DMA((4, 2, kv_heads)),
            pltpu.SemaphoreType.DMA((4,)),
            pltpu.SemaphoreType.DMA((4,)),
            pltpu.SemaphoreType.DMA((2, 2, kv_heads)),
            pltpu.SemaphoreType.DMA,
            pltpu.SemaphoreType.DMA((kv_heads,)),
        ],
        compiler_params=pltpu.CompilerParams(
            collective_id=0, has_side_effects=True, vmem_limit_bytes=48 * 1024 * 1024),
        cost_estimate=pl.CostEstimate(
            flops=flops, bytes_accessed=6 * rows * q_cols, transcendentals=8 * rows * 5 * TILE),
    )(queries, key_states, value_states, seg_tile)


def solution(mesh):
    in_specs = (
        P(("grp", "seq"), "head"),
        P(("grp", "seq"), "head"),
        P(("grp", "seq"), "head"),
        P(("grp", "seq")),
    )
    out_specs = P(("grp", "seq"), "head")
    return jax.shard_map(body, mesh=mesh, in_specs=in_specs, out_specs=out_specs, check_vma=False)
```

```python
import functools

import jax
import jax.numpy as jnp
from jax import lax
from jax.experimental import pallas as pl
from jax.experimental.pallas import tpu as pltpu
from jax.sharding import PartitionSpec as P

HEAD_DIM = 128
WINDOW = 1024
LANES = 128
TILE = 256
MESH = pl.DeviceIdType.MESH

SCALE2 = (168.0 ** (-0.5)) * 1.4426950408889634
NEG = -1e30

OWN_F, OWN_B, FP1, FP2, BN1, BN2, RELAY = range(7)


def kernel(n, relay, kv_heads, groups, q_hbm, k_hbm, v_hbm, seg_ref, o_hbm,
           kv, q_vm, o_vm, segs, lo,
           send_sem, recv_sem, seg_send, seg_recv, own_sem, q_sem, o_sem):
    me = lax.axis_index("seq")
    half = q_vm.shape[0] // 2
    rows_seg = half // LANES

    offsets = (1, 2, -1, -2)
    slots = (FP1, FP2, BN1, BN2)

    def exists(off):
        return (me + off >= 0) & (me + off < n)

    barrier = pltpu.get_barrier_semaphore()
    for off in offsets:
        @pl.when(exists(off))
        def _():
            pl.semaphore_signal(barrier, inc=1, device_id={"seq": me + off}, device_id_type=MESH)
    peers = sum(exists(off).astype(jnp.int32) for off in offsets)
    pl.semaphore_wait(barrier, peers)

    def seg_copy(j):
        return pltpu.make_async_remote_copy(
            src_ref=seg_ref, dst_ref=segs.at[j], send_sem=seg_send.at[j], recv_sem=seg_recv.at[j],
            device_id={"seq": me + offsets[j]}, device_id_type=MESH)

    def part(ref, row, h):
        return ref.at[pl.ds(row, half), pl.ds(pl.multiple_of(h * HEAD_DIM, HEAD_DIM), HEAD_DIM)]

    def kv_copy(j, which, h):
        return pltpu.make_async_remote_copy(
            src_ref=part((k_hbm, v_hbm)[which], 0 if j < 2 else half, h), dst_ref=kv.at[slots[j], which, h],
            send_sem=send_sem.at[j, which, h], recv_sem=recv_sem.at[j, which, h],
            device_id={"seq": me + offsets[j]}, device_id_type=MESH)

    def down_copy(which, h):
        return pltpu.make_async_remote_copy(
            src_ref=part((k_hbm, v_hbm)[which], 0, h), dst_ref=kv.at[RELAY, which, h],
            send_sem=send_sem.at[4, which, h], recv_sem=recv_sem.at[4, which, h],
            device_id={"seq": me - 1}, device_id_type=MESH)

    def relay_copy(which, h):
        return pltpu.make_async_remote_copy(
            src_ref=kv.at[RELAY, which, h], dst_ref=kv.at[FP1, which, h],
            send_sem=send_sem.at[5, which, h], recv_sem=recv_sem.at[0, which, h],
            device_id={"seq": me + 2}, device_id_type=MESH)

    odd = me % 2 == 1
    if relay:
        sends_down, gets_down = odd, jnp.logical_not(odd)
        relays = jnp.logical_not(odd) & (me + 2 < n)
        sends_up = jnp.logical_not(odd)
    else:
        sends_down, gets_down = me == n - 1, me == n - 2
        relays = None
        sends_up = me + 1 < n
    sends = (sends_up, exists(2), exists(-1), exists(-2))

    def each(condition, action):
        @pl.when(condition)
        def _():
            for which in range(2):
                action(which)

    def start_front(h):
        each(sends_down, lambda w: down_copy(w, h).start())
        for j in (0, 1):
            each(sends[j], lambda w: kv_copy(j, w, h).start())

    def start_back(h):
        for j in (2, 3):
            each(sends[j], lambda w: kv_copy(j, w, h).start())

    def wait_sends(h):
        each(sends_down, lambda w: down_copy(w, h).wait_send())
        for j in range(4):
            each(sends[j], lambda w: kv_copy(j, w, h).wait_send())
        if relay:
            each(relays, lambda w: relay_copy(w, h).wait_send())

    def own_copy(b, which, h):
        return pltpu.make_async_copy(
            part((k_hbm, v_hbm)[which], b * half, h), kv.at[b, which, h], own_sem.at[b, which, h])

    for j in range(4):
        @pl.when(exists(offsets[j]))
        def _():
            seg_copy(j).start()
    for h in range(min(2, kv_heads)):
        start_front(h)
        start_back(h)
    q_copy = pltpu.make_async_copy(q_hbm, q_vm, q_sem)
    q_copy.start()
    for h in range(kv_heads):
        for b in range(2):
            for which in range(2):
                own_copy(b, which, h).start()

    for slot, missing in ((FP1, me < 1), (FP2, me < 2)):
        @pl.when(missing)
        def _():
            kv[slot] = jnp.zeros(kv.shape[1:], kv.dtype)
            segs[slot - FP1] = jnp.full(segs.shape[1:], -1, segs.dtype)

    segs[4] = seg_ref[...]
    for j in range(4):
        there = exists(-offsets[j])

        @pl.when(there)
        def _():
            seg_copy(j).wait_recv()

    last = me == n - 1
    second = me == n - 2
    seg_places = (
        ((1, 0), (0, 0), (4, 0)),
        (
            (jnp.where(last, 0, jnp.where(second, 2, 3)), jnp.where(last | second, 0, rows_seg)),
            (jnp.where(last, 4, 2), jnp.where(last, 0, rows_seg)),
            (4, rows_seg),
        ),
    )
    for b in range(2):
        band = []
        for slot, row in seg_places[b]:
            for c in range(rows_seg):
                band.append(segs[slot, pl.ds(row + c, 1), :])
        for c in range(rows_seg):
            own = band[2 * rows_seg + c]
            own_col = jnp.transpose(jnp.broadcast_to(own, (LANES, LANES)))
            count = jnp.zeros((LANES, LANES), jnp.float32)
            for keys in band:
                count = count + jnp.where(keys < own_col, 1.0, 0.0)
            first = jnp.sum(count, axis=1, keepdims=True).astype(jnp.int32)
            row_of = lax.broadcasted_iota(jnp.int32, (LANES, LANES), 0) + (c * LANES + 1)
            lo[b, pl.ds(c * LANES, LANES), :] = jnp.maximum(jnp.broadcast_to(first, (LANES, LANES)), row_of)

    q_copy.wait()

    def out_copy(h):
        cols = pl.ds(pl.multiple_of(h * groups * HEAD_DIM, HEAD_DIM), groups * HEAD_DIM)
        return pltpu.make_async_copy(o_vm.at[:, cols], o_hbm.at[:, cols], o_sem.at[h])

    def attend(h, b, g):
        older1 = jnp.where(b == 0, FP1, jnp.where(last, OWN_F, BN1))
        older2 = jnp.where(b == 0, FP2, jnp.where(last, FP1, jnp.where(second, RELAY, BN2)))
        col = pl.multiple_of((h * groups + g) * HEAD_DIM, HEAD_DIM)
        for t in range(half // TILE):
            row = pl.multiple_of(b * half + t * TILE, TILE)
            q = q_vm[pl.ds(row, TILE), pl.ds(col, HEAD_DIM)]
            low = lo[b, pl.ds(t * TILE, TILE), 0:1]
            pieces = (
                (older2, t * TILE, half - t * TILE, t * TILE),
                (older1, 0, half, half),
                (b, 0, (t + 1) * TILE, 2 * half),
            )
            scores = []
            for p, (slot, k0, kn, base) in enumerate(pieces):
                k = kv[slot, 0, h, pl.ds(k0, kn), :]
                s = lax.dot_general(q, k, (((1,), (1,)), ((), ())), preferred_element_type=jnp.float32)
                key_at = lax.broadcasted_iota(jnp.int32, (TILE, kn), 1) + base
                seen = key_at >= low
                if p == 2:
                    row_at = lax.broadcasted_iota(jnp.int32, (TILE, kn), 0) + (2 * half + t * TILE)
                    seen = seen & (key_at <= row_at)
                scores.append(jnp.where(seen, s * SCALE2, NEG))
            top = functools.reduce(jnp.maximum, [jnp.max(s, axis=1, keepdims=True) for s in scores])
            acc = None
            for s, (slot, k0, kn, base) in zip(scores, pieces):
                w = jnp.exp2(s - top).astype(jnp.bfloat16)
                v = kv[slot, 1, h, pl.ds(k0, kn), :]
                v = jnp.concatenate([v, jnp.ones((kn, LANES), jnp.bfloat16)], axis=1)
                d = lax.dot_general(w, v, (((1,), (0,)), ((), ())), preferred_element_type=jnp.float32)
                acc = d if acc is None else acc + d
            o_vm[pl.ds(row, TILE), pl.ds(col, HEAD_DIM)] = (
                acc[:, :HEAD_DIM] / acc[:, HEAD_DIM:]).astype(o_vm.dtype)

    def head_step(h, carry):
        each(gets_down, lambda w: down_copy(w, h).wait_recv())
        if relay:
            each(relays, lambda w: relay_copy(w, h).start())
        for b in range(2):
            for which in range(2):
                own_copy(b, which, h).wait()
        each(me >= 1, lambda w: kv_copy(0, w, h).wait_recv())
        each(me >= 2, lambda w: kv_copy(1, w, h).wait_recv())

        @pl.when(h + 2 < kv_heads)
        def _():
            start_front(h + 2)

        for g in range(groups):
            attend(h, 0, g)
        each(me <= n - 2, lambda w: kv_copy(2, w, h).wait_recv())
        each(me <= n - 3, lambda w: kv_copy(3, w, h).wait_recv())

        @pl.when(h + 2 < kv_heads)
        def _():
            start_back(h + 2)

        for g in range(groups):
            attend(h, 1, g)
        out_copy(h).start()
        return carry

    lax.fori_loop(0, kv_heads, head_step, 0)

    for j in range(4):
        @pl.when(exists(offsets[j]))
        def _():
            seg_copy(j).wait_send()

    def finish(h, carry):
        wait_sends(h)
        out_copy(h).wait()
        return carry

    lax.fori_loop(0, kv_heads, finish, 0)


def body(queries, key_states, value_states, segment_ids):
    rows, q_cols = queries.shape
    half = rows // 2
    kv_heads = key_states.shape[1] // HEAD_DIM
    groups = q_cols // key_states.shape[1]
    n = lax.axis_size("seq")
    relay = n == 8
    seg_tile = segment_ids.reshape(rows // LANES, LANES)
    anywhere = pl.BlockSpec(memory_space=pl.ANY)
    flops = 4 * rows * q_cols * 5 * TILE
    return pl.pallas_call(
        functools.partial(kernel, n, relay, kv_heads, groups),
        out_shape=jax.ShapeDtypeStruct((rows, q_cols), jnp.bfloat16),
        in_specs=[anywhere, anywhere, anywhere, pl.BlockSpec(memory_space=pltpu.VMEM)],
        out_specs=anywhere,
        scratch_shapes=[
            pltpu.VMEM((7, 2, kv_heads, half, HEAD_DIM), jnp.bfloat16),
            pltpu.VMEM((rows, q_cols), jnp.bfloat16),
            pltpu.VMEM((rows, q_cols), jnp.bfloat16),
            pltpu.VMEM((5, rows // LANES, LANES), jnp.int32),
            pltpu.VMEM((2, half, LANES), jnp.int32),
            pltpu.SemaphoreType.DMA((6, 2, kv_heads)),
            pltpu.SemaphoreType.DMA((5, 2, kv_heads)),
            pltpu.SemaphoreType.DMA((4,)),
            pltpu.SemaphoreType.DMA((4,)),
            pltpu.SemaphoreType.DMA((2, 2, kv_heads)),
            pltpu.SemaphoreType.DMA,
            pltpu.SemaphoreType.DMA((kv_heads,)),
        ],
        compiler_params=pltpu.CompilerParams(
            collective_id=0, has_side_effects=True, vmem_limit_bytes=60 * 1024 * 1024),
        cost_estimate=pl.CostEstimate(
            flops=flops, bytes_accessed=6 * rows * q_cols, transcendentals=8 * rows * 5 * TILE),
    )(queries, key_states, value_states, seg_tile)


def solution(mesh):
    in_specs = (
        P(("grp", "seq"), "head"),
        P(("grp", "seq"), "head"),
        P(("grp", "seq"), "head"),
        P(("grp", "seq")),
    )
    out_specs = P(("grp", "seq"), "head")
    return jax.shard_map(body, mesh=mesh, in_specs=in_specs, out_specs=out_specs, check_vma=False)
```

```python
import functools

import jax
import jax.numpy as jnp
from jax import lax
from jax.experimental import pallas as pl
from jax.experimental.pallas import tpu as pltpu
from jax.sharding import PartitionSpec as P

HEAD_DIM = 128
WINDOW = 1024
LANES = 128
TILE = 256
MESH = pl.DeviceIdType.MESH

SCALE2 = (168.0 ** (-0.5)) * 1.4426950408889634
NEG = -1e30

OWN_F, OWN_B, FP1, FP2, BN1, BN2, RELAY = range(7)


def kernel(n, relay, kv_heads, groups, q_hbm, k_hbm, v_hbm, seg_ref, o_vm,
           kv, q_vm, segs, lo,
           send_sem, recv_sem, seg_send, seg_recv, own_sem, q_sem):
    me = lax.axis_index("seq")
    half = q_vm.shape[0] // 2
    rows_seg = half // LANES

    offsets = (1, 2, -1, -2)
    slots = (FP1, FP2, BN1, BN2)

    def exists(off):
        return (me + off >= 0) & (me + off < n)

    barrier = pltpu.get_barrier_semaphore()
    for off in offsets:
        @pl.when(exists(off))
        def _():
            pl.semaphore_signal(barrier, inc=1, device_id={"seq": me + off}, device_id_type=MESH)
    peers = sum(exists(off).astype(jnp.int32) for off in offsets)
    pl.semaphore_wait(barrier, peers)

    def seg_copy(j):
        return pltpu.make_async_remote_copy(
            src_ref=seg_ref, dst_ref=segs.at[j], send_sem=seg_send.at[j], recv_sem=seg_recv.at[j],
            device_id={"seq": me + offsets[j]}, device_id_type=MESH)

    def part(ref, row, h):
        return ref.at[pl.ds(row, half), pl.ds(pl.multiple_of(h * HEAD_DIM, HEAD_DIM), HEAD_DIM)]

    def kv_copy(j, which, h):
        return pltpu.make_async_remote_copy(
            src_ref=part((k_hbm, v_hbm)[which], 0 if j < 2 else half, h), dst_ref=kv.at[slots[j], which, h],
            send_sem=send_sem.at[j, which, h], recv_sem=recv_sem.at[j, which, h],
            device_id={"seq": me + offsets[j]}, device_id_type=MESH)

    def down_copy(which, h):
        return pltpu.make_async_remote_copy(
            src_ref=part((k_hbm, v_hbm)[which], 0, h), dst_ref=kv.at[RELAY, which, h],
            send_sem=send_sem.at[4, which, h], recv_sem=recv_sem.at[4, which, h],
            device_id={"seq": me - 1}, device_id_type=MESH)

    def relay_copy(which, h):
        return pltpu.make_async_remote_copy(
            src_ref=kv.at[RELAY, which, h], dst_ref=kv.at[FP1, which, h],
            send_sem=send_sem.at[5, which, h], recv_sem=recv_sem.at[0, which, h],
            device_id={"seq": me + 2}, device_id_type=MESH)

    odd = me % 2 == 1
    if relay:
        sends_down, gets_down = odd, jnp.logical_not(odd)
        relays = jnp.logical_not(odd) & (me + 2 < n)
        sends_up = jnp.logical_not(odd)
    else:
        sends_down, gets_down = me == n - 1, me == n - 2
        relays = None
        sends_up = me + 1 < n
    sends = (sends_up, exists(2), exists(-1), exists(-2))

    def each(condition, action):
        @pl.when(condition)
        def _():
            for which in range(2):
                action(which)

    def start_front(h):
        each(sends_down, lambda w: down_copy(w, h).start())
        for j in (0, 1):
            each(sends[j], lambda w: kv_copy(j, w, h).start())

    def start_back(h):
        for j in (2, 3):
            each(sends[j], lambda w: kv_copy(j, w, h).start())

    def wait_sends(h):
        each(sends_down, lambda w: down_copy(w, h).wait_send())
        for j in range(4):
            each(sends[j], lambda w: kv_copy(j, w, h).wait_send())
        if relay:
            each(relays, lambda w: relay_copy(w, h).wait_send())

    def own_copy(b, which, h):
        return pltpu.make_async_copy(
            part((k_hbm, v_hbm)[which], b * half, h), kv.at[b, which, h], own_sem.at[b, which, h])

    for j in range(4):
        @pl.when(exists(offsets[j]))
        def _():
            seg_copy(j).start()
    for h in range(min(2, kv_heads)):
        start_front(h)
        start_back(h)
    q_copy = pltpu.make_async_copy(q_hbm, q_vm, q_sem)
    q_copy.start()
    for h in range(kv_heads):
        for b in range(2):
            for which in range(2):
                own_copy(b, which, h).start()

    for slot, missing in ((FP1, me < 1), (FP2, me < 2)):
        @pl.when(missing)
        def _():
            kv[slot] = jnp.zeros(kv.shape[1:], kv.dtype)
            segs[slot - FP1] = jnp.full(segs.shape[1:], -1, segs.dtype)

    segs[4] = seg_ref[...]
    for j in range(4):
        there = exists(-offsets[j])

        @pl.when(there)
        def _():
            seg_copy(j).wait_recv()

    last = me == n - 1
    second = me == n - 2
    seg_places = (
        ((1, 0), (0, 0), (4, 0)),
        (
            (jnp.where(last, 0, jnp.where(second, 2, 3)), jnp.where(last | second, 0, rows_seg)),
            (jnp.where(last, 4, 2), jnp.where(last, 0, rows_seg)),
            (4, rows_seg),
        ),
    )
    for b in range(2):
        band = []
        for slot, row in seg_places[b]:
            for c in range(rows_seg):
                band.append(segs[slot, pl.ds(row + c, 1), :])
        for c in range(rows_seg):
            own = band[2 * rows_seg + c]
            own_col = jnp.transpose(jnp.broadcast_to(own, (LANES, LANES)))
            count = jnp.zeros((LANES, LANES), jnp.float32)
            for keys in band:
                count = count + jnp.where(keys < own_col, 1.0, 0.0)
            first = jnp.sum(count, axis=1, keepdims=True).astype(jnp.int32)
            row_of = lax.broadcasted_iota(jnp.int32, (LANES, LANES), 0) + (c * LANES + 1)
            lo[b, pl.ds(c * LANES, LANES), :] = jnp.maximum(jnp.broadcast_to(first, (LANES, LANES)), row_of)

    q_copy.wait()

    def attend(h, b, g):
        older1 = jnp.where(b == 0, FP1, jnp.where(last, OWN_F, BN1))
        older2 = jnp.where(b == 0, FP2, jnp.where(last, FP1, jnp.where(second, RELAY, BN2)))
        col = pl.multiple_of((h * groups + g) * HEAD_DIM, HEAD_DIM)
        for t in range(half // TILE):
            row = pl.multiple_of(b * half + t * TILE, TILE)
            q = q_vm[pl.ds(row, TILE), pl.ds(col, HEAD_DIM)]
            low = lo[b, pl.ds(t * TILE, TILE), 0:1]
            pieces = (
                (older2, t * TILE, half - t * TILE, t * TILE),
                (older1, 0, half, half),
                (b, 0, (t + 1) * TILE, 2 * half),
            )
            scores = []
            for p, (slot, k0, kn, base) in enumerate(pieces):
                k = kv[slot, 0, h, pl.ds(k0, kn), :]
                s = lax.dot_general(q, k, (((1,), (1,)), ((), ())), preferred_element_type=jnp.float32)
                key_at = lax.broadcasted_iota(jnp.int32, (TILE, kn), 1) + base
                seen = key_at >= low
                if p == 2:
                    row_at = lax.broadcasted_iota(jnp.int32, (TILE, kn), 0) + (2 * half + t * TILE)
                    seen = seen & (key_at <= row_at)
                scores.append(jnp.where(seen, s * SCALE2, NEG))
            top = functools.reduce(jnp.maximum, [jnp.max(s, axis=1, keepdims=True) for s in scores])
            acc = None
            for s, (slot, k0, kn, base) in zip(scores, pieces):
                w = jnp.exp2(s - top).astype(jnp.bfloat16)
                v = kv[slot, 1, h, pl.ds(k0, kn), :]
                v = jnp.concatenate([v, jnp.ones((kn, LANES), jnp.bfloat16)], axis=1)
                d = lax.dot_general(w, v, (((1,), (0,)), ((), ())), preferred_element_type=jnp.float32)
                acc = d if acc is None else acc + d
            o_vm[pl.ds(row, TILE), pl.ds(col, HEAD_DIM)] = (
                acc[:, :HEAD_DIM] / acc[:, HEAD_DIM:]).astype(o_vm.dtype)

    def pass_on(h):
        each(gets_down, lambda w: down_copy(w, h).wait_recv())
        if relay:
            each(relays, lambda w: relay_copy(w, h).start())

    def head_step(h, carry):
        for b in range(2):
            for which in range(2):
                own_copy(b, which, h).wait()
        each(me >= 1, lambda w: kv_copy(0, w, h).wait_recv())
        each(me >= 2, lambda w: kv_copy(1, w, h).wait_recv())

        @pl.when(h + 2 < kv_heads)
        def _():
            start_front(h + 2)

        for g in range(groups):
            attend(h, 0, g)
        each(me <= n - 2, lambda w: kv_copy(2, w, h).wait_recv())
        each(me <= n - 3, lambda w: kv_copy(3, w, h).wait_recv())

        @pl.when(h + 2 < kv_heads)
        def _():
            start_back(h + 2)

        @pl.when(h + 1 < kv_heads)
        def _():
            pass_on(h + 1)

        for g in range(groups):
            attend(h, 1, g)
        return carry

    pass_on(0)
    lax.fori_loop(0, kv_heads, head_step, 0)

    for j in range(4):
        @pl.when(exists(offsets[j]))
        def _():
            seg_copy(j).wait_send()

    def finish(h, carry):
        wait_sends(h)
        return carry

    lax.fori_loop(0, kv_heads, finish, 0)


def body(queries, key_states, value_states, segment_ids):
    rows, q_cols = queries.shape
    half = rows // 2
    kv_heads = key_states.shape[1] // HEAD_DIM
    groups = q_cols // key_states.shape[1]
    n = lax.axis_size("seq")
    relay = n == 8
    seg_tile = segment_ids.reshape(rows // LANES, LANES)
    anywhere = pl.BlockSpec(memory_space=pl.ANY)
    flops = 4 * rows * q_cols * 5 * TILE
    return pl.pallas_call(
        functools.partial(kernel, n, relay, kv_heads, groups),
        out_shape=pltpu.VMEM((rows, q_cols), jnp.bfloat16),
        in_specs=[anywhere, anywhere, anywhere, pl.BlockSpec(memory_space=pltpu.VMEM)],
        out_specs=pl.BlockSpec(memory_space=pltpu.VMEM),
        scratch_shapes=[
            pltpu.VMEM((7, 2, kv_heads, half, HEAD_DIM), jnp.bfloat16),
            pltpu.VMEM((rows, q_cols), jnp.bfloat16),
            pltpu.VMEM((5, rows // LANES, LANES), jnp.int32),
            pltpu.VMEM((2, half, LANES), jnp.int32),
            pltpu.SemaphoreType.DMA((6, 2, kv_heads)),
            pltpu.SemaphoreType.DMA((5, 2, kv_heads)),
            pltpu.SemaphoreType.DMA((4,)),
            pltpu.SemaphoreType.DMA((4,)),
            pltpu.SemaphoreType.DMA((2, 2, kv_heads)),
            pltpu.SemaphoreType.DMA,
        ],
        compiler_params=pltpu.CompilerParams(
            collective_id=0, has_side_effects=True, vmem_limit_bytes=60 * 1024 * 1024),
        cost_estimate=pl.CostEstimate(
            flops=flops, bytes_accessed=6 * rows * q_cols, transcendentals=8 * rows * 5 * TILE),
    )(queries, key_states, value_states, seg_tile)


def solution(mesh):
    in_specs = (
        P(("grp", "seq"), "head"),
        P(("grp", "seq"), "head"),
        P(("grp", "seq"), "head"),
        P(("grp", "seq")),
    )
    out_specs = P(("grp", "seq"), "head")
    return jax.shard_map(body, mesh=mesh, in_specs=in_specs, out_specs=out_specs, check_vma=False)
```
